256 devices in a mesh: ops: 4 (over x_lo, core), sec: 64 (over y, x_hi, z).
Axes of the slice: x: 4 (x_hi: 2, x_lo: 2; x = x_hi * 2 + x_lo), y: 4, z: 8, core: 2. Of those that a mesh axis runs over, the one named last changes fastest.
Arguments:
- wavefunction: bfloat16 [2, 256, 256, 256], P(None, 'sec')
- left_blocks: bfloat16 [40, 256, 256, 256], P('ops', 'sec'), may hold values from -0.0625 to 0.0625
- right_blocks: bfloat16 [40, 256, 256, 256], P('ops', 'sec'), may hold values from -0.375 to 0.375
- pairing: int32 [40, 256], P('ops', 'sec'), may hold values from 0 to 255, as said below
- sector_dims: int32 [2, 256], replicated, may hold values from 1 to 256, as said below
Outputs:
- sigma: float32 [2, 256, 256, 256], P(None, 'sec', 'ops')
The draws below stay inside these ranges and needn't reach their ends.
Inputs may be any that keep to these rules, and one draw needn't show every extreme that they name: pairing[t, l] differs from l by at most 4, and by exactly 4 for some term. `sector_dims`: each side has some sector of dimension 256.
All inputs are finite; a program needn't handle non-finite values.
Results may differ from the reference program's by a relative error of at most 0.0029.
Values sent between devices are 32-bit elements; how exact they have to be, the bound alone decides.
No kernel may reach another device: no remote copies, remote signals or barrier semaphores. Data moves between devices by JAX's collectives and lax.ppermute only.
A program may use at most 192 MiB of HBM per device.

```python
import jax
import jax.numpy as jnp
from jax import lax

PAD = 256
SEC_DEV = 4
NSEC = 256
TERMS = 40


def draw_wavefunction(key, part):
    key = jax.random.fold_in(key, 11)
    first_key, second_key = jax.random.split(key)
    sector_ids = jnp.arange(NSEC, dtype=jnp.float32)
    ramp = 1.0 + 2.0 * sector_ids / max(NSEC - 1, 1)
    base_values = jnp.clip(jax.random.normal(first_key, (2, NSEC, PAD, PAD), jnp.float32), -4.0, 4.0)
    block_scale = jnp.exp(jax.random.uniform(second_key, (2, NSEC), jnp.float32, -0.7, 0.7))
    scaled = base_values * ramp[None, :, None, None] * block_scale[:, :, None, None]
    return scaled.astype(jnp.bfloat16)


def draw_pairing(key, part):
    key = jax.random.fold_in(key, 12)
    first_key, second_key = jax.random.split(key)
    offsets = jax.random.randint(first_key, (TERMS, NSEC), -SEC_DEV, SEC_DEV + 1)
    chosen_term = jax.random.randint(second_key, (), 0, TERMS)
    sector_ids = jnp.arange(NSEC, dtype=jnp.int32)
    forced = jnp.where(sector_ids % 2 == 0, SEC_DEV, -SEC_DEV)
    term_ids = jnp.arange(TERMS, dtype=jnp.int32)
    offsets = jnp.where(term_ids[:, None] == chosen_term, forced[None, :], offsets)
    return jnp.clip(sector_ids[None, :] + offsets, 0, NSEC - 1).astype(jnp.int32)


def draw_sector_dims(key, part):
    key = jax.random.fold_in(key, 13)
    first_key, second_key, third_key = jax.random.split(key, 3)
    dimensions = jax.random.randint(first_key, (2, NSEC), 1, PAD + 1)
    widest = jax.random.randint(second_key, (2,), 0, NSEC)
    narrowest = (widest + 1 + jax.random.randint(third_key, (2,), 0, NSEC - 1)) % NSEC
    sector_ids = jnp.arange(NSEC, dtype=jnp.int32)
    dimensions = jnp.where(sector_ids[None, :] == widest[:, None], PAD, dimensions)
    dimensions = jnp.where(sector_ids[None, :] == narrowest[:, None], 1, dimensions)
    return dimensions.astype(jnp.int32)


def levels(stream_key, extent, cuts, least, top_value):
    level, own = 1.0, jax.random.fold_in(stream_key, 6)
    for axis_at, shards_of in cuts:
        heights = jnp.exp(jax.random.uniform(jax.random.fold_in(own, axis_at), (shards_of,), jnp.float32, least / len(cuts), top_value / len(cuts)))
        level = level * jnp.repeat(heights, extent[axis_at] // shards_of).reshape([-1 if axis == axis_at else 1 for axis in range(len(extent))])
    return level


def gaussian(rng, extent, spread, bound, cuts=(), held_as=jnp.bfloat16):
    gain = levels(rng, extent, cuts, -0.22, 0.18) if cuts else 1.0
    drawn = jax.random.normal(rng, extent, jnp.float32) * spread * gain
    return jnp.minimum(jnp.maximum(drawn, -bound), bound).astype(held_as)


def setup_inputs(seed: int = 0) -> dict:
    key_of = jax.random.split(jax.random.key(seed), 6)
    return {
        "wavefunction": draw_wavefunction(jax.random.fold_in(key_of[5], 71), 0),
        "left_blocks": gaussian(key_of[1], (TERMS, NSEC, PAD, PAD), (PAD * TERMS) ** -0.5, 0.0625, ((0, 4), (1, 64))),
        "right_blocks": gaussian(key_of[2], (TERMS, NSEC, PAD, PAD), PAD ** -0.5, 0.375, ((0, 4), (1, 64))),
        "pairing": draw_pairing(jax.random.fold_in(key_of[5], 71), 0),
        "sector_dims": draw_sector_dims(jax.random.fold_in(key_of[5], 71), 0),
    }


def reference(wavefunction, left_blocks, right_blocks, pairing, sector_dims):
    row_ids = jnp.arange(PAD, dtype=jnp.int32)
    left_mask = row_ids[None, :] < sector_dims[0][:, None]
    right_mask = row_ids[None, :] < sector_dims[1][:, None]
    valid_mask = left_mask[:, :, None] & right_mask[:, None, :]
    masked = jnp.where(valid_mask[None], wavefunction, jnp.zeros((), wavefunction.dtype))

    def sector_step(accumulated, sector):
        sender_device = masked[:, sector].astype(jnp.float32)
        left_factor = left_blocks[:, sector].astype(jnp.float32)
        right_factor = right_blocks[:, sector].astype(jnp.float32)
        partial_product = jnp.einsum('jmx,hfx->jhmf', sender_device, right_factor).astype(jnp.bfloat16)
        term_contribution = jnp.einsum('mos,nmsd->nmod', left_factor, partial_product.astype(jnp.float32))
        accumulated = accumulated.at[:, pairing[:, sector]].add(term_contribution)
        return accumulated, None

    start_sum = jnp.zeros((2, NSEC, PAD, PAD), jnp.float32)
    accumulated, unused = lax.scan(sector_step, start_sum, jnp.arange(NSEC, dtype=jnp.int32))
    return jnp.where(valid_mask[None], accumulated, jnp.zeros((), jnp.float32))
```

```python
import functools

import jax
import jax.numpy as jnp
from jax import lax
from jax.experimental import pallas as pl
from jax.experimental.pallas import tpu as pltpu
from jax.sharding import PartitionSpec as P

Z_RUN = 8
BOTH = ("ops", "sec")
UNROLL = 5


def terms_kernel(
    vectors, halo, me_ref, dims_hbm, pair_hbm, wave_ref, left_ref, right_ref, *refs
):
    number = len(vectors)
    keep_refs, send_refs = refs[: 2 * number : 2], refs[1 : 2 * number : 2]
    (
        wave_buf, masked, left_buf, right_buf, half, dims_ref, pair_ref, code_ref,
        wave_sem, left_sem, right_sem, dims_sem, pair_sem,
    ) = refs[2 * number :]
    terms, sectors, pad, _ = left_ref.shape
    pairs = terms * sectors
    run = pad // 4
    peers = dims_ref.shape[1] // sectors
    me = me_ref[0]
    sec, ops = me % peers, me // peers
    core, x_lo = ops % 2, ops // 2
    first = sec * sectors
    z = sec % Z_RUN

    dims_copy = pltpu.make_async_copy(dims_hbm, dims_ref, dims_sem)
    pair_copy = pltpu.make_async_copy(pair_hbm, pair_ref, pair_sem)
    pair_copy.start()
    dims_copy.start()
    wave_copies = [
        pltpu.make_async_copy(wave_ref.at[v], wave_buf.at[j], wave_sem.at[j])
        for j, v in enumerate(vectors)
    ]
    for copy in wave_copies:
        copy.start()
    for keep_ref, send_ref in zip(keep_refs, send_refs):
        keep_ref[...] = jnp.zeros_like(keep_ref)
        send_ref[...] = jnp.zeros_like(send_ref)
    left_buf[pairs] = jnp.zeros((pad, pad), jnp.bfloat16)
    right_buf[pairs] = jnp.zeros((pad, pad), jnp.bfloat16)
    pair_copy.wait()

    def left_copy(t, l, i):
        return pltpu.make_async_copy(left_ref.at[t, l], left_buf.at[i], left_sem.at[i])

    def right_copy(t, l, i):
        return pltpu.make_async_copy(right_ref.at[t, l], right_buf.at[i], right_sem.at[i])

    def scan(t, count):
        for l in range(sectors):
            place = pair_ref[l, t] - first
            outside = (place < 0) | (place >= sectors)
            take = outside if halo else jnp.logical_not(outside)

            @pl.when(take)
            def _():
                code_ref[count] = count * 1024 + l * 64 + place + sectors
                right_copy(t, l, count).start()
                left_copy(t, l, count).start()

            count = count + take.astype(jnp.int32)
        return count

    count = lax.fori_loop(0, terms, scan, jnp.int32(0))
    for u in range(UNROLL - 1):
        code_ref[count + u] = pairs * 1024 + sectors

    dims_copy.wait()
    for copy in wave_copies:
        copy.wait()
    rows = lax.broadcasted_iota(jnp.int32, (pad, pad), 0)
    cols = lax.broadcasted_iota(jnp.int32, (pad, pad), 1)
    for l in range(sectors):
        valid = (rows < dims_ref[0, first + l]) & (cols < dims_ref[1, first + l])
        for j in range(number):
            value = jnp.where(valid, wave_buf[j, l].astype(jnp.float32), 0.0)
            masked[l, j * pad : (j + 1) * pad] = value.astype(jnp.bfloat16)

    def first_stage(u, i):
        code = code_ref[i]
        product = lax.dot_general(
            masked[code % 1024 // 64], right_buf[code // 1024], (((1,), (1,)), ((), ())),
            preferred_element_type=jnp.float32,
        )
        half[u] = product.astype(jnp.bfloat16)

    def second_stage(u, i):
        code = code_ref[i]
        place = code % 64 - sectors
        if halo:
            at = jnp.where(place < 0, place + sectors, place)
            flip = jnp.where(place < 0, z == 0, z == Z_RUN - 1).astype(jnp.int32)
        else:
            at, flip = place, 0
        near = x_lo ^ flip
        blocks = [2 * near + core, 2 * (1 - near) + core, 2 * near + 1 - core, 2 * (1 - near) + 1 - core]
        lhs = jnp.concatenate(
            [left_buf[code // 1024, pl.ds(pl.multiple_of(b * run, run), run), :] for b in blocks], axis=0
        )
        for j in range(number):
            term = lax.dot_general(
                lhs, half[u, j * pad : (j + 1) * pad], (((1,), (0,)), ((), ())),
                preferred_element_type=jnp.float32,
            )
            for q in range(2):
                keep_refs[j][q, at] += term[q * run : (q + 1) * run]
                send_refs[j][q, at] += term[(2 + q) * run : (3 + q) * run]

    def step(k, carry):
        base = k * UNROLL
        for u in range(UNROLL):

            @pl.when(base + u < count)
            def _():
                right_copy(0, 0, base + u).wait()
                left_copy(0, 0, base + u).wait()

        first_stage(0, base)
        for u in range(UNROLL):
            if u + 1 < UNROLL:
                first_stage(u + 1, base + u + 1)
            second_stage(u, base + u)
        return carry

    lax.fori_loop(0, (count + UNROLL - 1) // UNROLL, step, 0)


def terms_call(vectors, halo, me, dims, pairing, wave, left, right):
    terms, sectors, pad, _ = left.shape
    number = len(vectors)
    pairs = terms * sectors
    places = 2 * sectors if halo else sectors
    shape = jax.ShapeDtypeStruct((2, places, pad // 4, pad), jnp.float32)
    in_hbm = pl.BlockSpec(memory_space=pltpu.HBM)
    vmem = pl.BlockSpec(memory_space=pltpu.VMEM)
    operands = (dims, pairing.T, wave, left, right)
    return pl.pallas_call(
        functools.partial(terms_kernel, vectors, halo),
        out_shape=(shape,) * (2 * number),
        in_specs=[pl.BlockSpec(memory_space=pltpu.SMEM)] + [in_hbm] * 5,
        out_specs=(vmem,) * (2 * number),
        scratch_shapes=[
            pltpu.VMEM((number, sectors, pad, pad), jnp.bfloat16),
            pltpu.VMEM((sectors, number * pad, pad), jnp.bfloat16),
            pltpu.VMEM((pairs + 1, pad, pad), jnp.bfloat16),
            pltpu.VMEM((pairs + 1, pad, pad), jnp.bfloat16),
            pltpu.VMEM((UNROLL, number * pad, pad), jnp.bfloat16),
            pltpu.SMEM(dims.shape, jnp.int32),
            pltpu.SMEM((sectors, terms), jnp.int32),
            pltpu.SMEM((pairs + UNROLL - 1,), jnp.int32),
            pltpu.SemaphoreType.DMA((number,)),
            pltpu.SemaphoreType.DMA((pairs,)),
            pltpu.SemaphoreType.DMA((pairs,)),
            pltpu.SemaphoreType.DMA,
            pltpu.SemaphoreType.DMA,
        ],
        compiler_params=pltpu.CompilerParams(vmem_limit_bytes=32 * 1024 * 1024),
        cost_estimate=pl.CostEstimate(
            flops=pairs // 2 * number * 4 * pad**3, bytes_accessed=pairs * pad * pad * 2, transcendentals=0
        ),
        name="halo_terms" if halo else "own_terms",
    )(me.reshape(1), *(pltpu.with_memory_space_constraint(x, pltpu.HBM) for x in operands))


def body(wavefunction, left_blocks, right_blocks, pairing, sector_dims):
    sectors, pad = wavefunction.shape[1:3]
    ops, sec = lax.axis_index("ops"), lax.axis_index("sec")
    peers = lax.axis_size("sec")
    other_core = [(i, i ^ 1) for i in range(4)]
    other_chip = [(i, i ^ 2) for i in range(4)]
    upward = [
        (o * peers + s, (o ^ 2 if s % Z_RUN == Z_RUN - 1 else o) * peers + (s + 1) % peers)
        for o in range(4)
        for s in range(peers)
    ]
    downward = [(b, a) for a, b in upward]

    def terms(vectors, halo, pairing):
        return terms_call(
            vectors, halo, lax.axis_index(BOTH), sector_dims, pairing, wavefunction, left_blocks, right_blocks
        )

    def to_core(x):
        return lax.ppermute(x, "ops", other_core)

    def to_chip(x):
        return lax.ppermute(x, "ops", other_chip)

    keep0, send0, keep1, send1 = terms((0, 1), True, pairing)
    recv0 = to_core(send0)
    recv1 = to_core(send1)
    halo0 = keep0 + recv0
    far1 = keep1[1] + recv1[1]
    halo0, far1, pairing_later = lax.optimization_barrier((halo0, far1, pairing))
    down0, up0 = halo0[:, :sectors], halo0[:, sectors:]
    below0 = lax.ppermute(up0, BOTH, upward)
    above0 = lax.ppermute(down0, BOTH, downward)
    far1 = to_chip(far1)
    halo1 = keep1[0] + recv1[0] + far1
    below1 = lax.ppermute(halo1[sectors:], BOTH, upward)
    above1 = lax.ppermute(halo1[:sectors], BOTH, downward)

    own0, give0, own1, give1 = terms((0, 1), False, pairing_later)
    got1 = to_core(give1)
    got0 = to_core(give0)
    own_far1 = to_chip(own1[1] + got1[1])
    far0 = to_chip(own0[1] + got0[1] + below0[1] + above0[1])
    out0 = own0[0] + got0[0] + below0[0] + above0[0] + far0
    out1 = own1[0] + got1[0] + own_far1 + below1 + above1

    local_dims = lax.dynamic_slice_in_dim(sector_dims, sec * sectors, sectors, 1)
    share_ids = ops * (pad // 4) + jnp.arange(pad // 4, dtype=jnp.int32)
    col_ids = jnp.arange(pad, dtype=jnp.int32)
    valid = (share_ids[None, :, None] < local_dims[0][:, None, None]) & (
        col_ids[None, None, :] < local_dims[1][:, None, None]
    )
    return jnp.where(valid[None], jnp.stack([out0, out1]), jnp.zeros((), jnp.float32))


def solution(mesh):
    placed = (
        P(None, "sec", None, None),
        P("ops", "sec", None, None),
        P("ops", "sec", None, None),
        P("ops", "sec"),
        P(),
    )
    return jax.shard_map(
        body, mesh=mesh, in_specs=placed, out_specs=P(None, "sec", "ops", None), check_vma=False
    )
```

```python
import functools

import jax
import jax.numpy as jnp
from jax import lax
from jax.experimental import pallas as pl
from jax.experimental.pallas import tpu as pltpu
from jax.sharding import PartitionSpec as P

Z_RUN = 8
BOTH = ("ops", "sec")
EARLY = 2
NT = (((1,), (1,)), ((), ()))
NN = (((1,), (0,)), ((), ()))


def terms_kernel(
    me_ref, dims_hbm, pair_hbm, wave_ref, left_ref, right_ref,
    keep0, send0, keep1, send1, inside,
    wave_buf, masked, left_buf, right_buf, half, dims_ref, pair_ref,
    wave_sem, left_sem, right_sem, dims_sem, pair_sem,
):
    terms, sectors, pad, _ = left_ref.shape
    run = pad // 4
    peers = dims_ref.shape[1] // sectors
    me = me_ref[0]
    sec, ops = me % peers, me // peers
    core, x_lo = ops % 2, ops // 2
    first = sec * sectors
    z = sec % Z_RUN

    pair_copy = pltpu.make_async_copy(pair_hbm, pair_ref, pair_sem)
    dims_copy = pltpu.make_async_copy(dims_hbm, dims_ref, dims_sem)
    parts = [(0, 0, EARLY), (0, EARLY, terms - EARLY)] + [(l, 0, terms) for l in range(1, sectors)]

    def wave_copy(l):
        return pltpu.make_async_copy(wave_ref.at[:, l], wave_buf.at[:, l], wave_sem.at[l])

    def right_copy(i):
        l, t, number = parts[i]
        at = pl.ds(t, number)
        return pltpu.make_async_copy(right_ref.at[at, l], right_buf.at[l, at], right_sem.at[i])

    def left_copy(i):
        l, t, number = parts[i]
        at = pl.ds(t, number)
        return pltpu.make_async_copy(left_ref.at[at, l], left_buf.at[l, at], left_sem.at[i])

    dims_copy.start()
    pair_copy.start()
    wave_copy(0).start()
    right_copy(0).start()
    left_copy(0).start()
    for i in range(1, len(parts)):
        if i < sectors:
            wave_copy(i).start(priority=1)
        right_copy(i).start(priority=1)
        left_copy(i).start(priority=1)

    for ref in (keep0, send0, keep1, send1):
        ref[...] = jnp.zeros_like(ref)
    rows = lax.broadcasted_iota(jnp.int32, (pad, pad), 0)
    cols = lax.broadcasted_iota(jnp.int32, (pad, pad), 1)

    def mask(l):
        valid = (rows < dims_ref[0, first + l]) & (cols < dims_ref[1, first + l])
        for v in range(2):
            value = jnp.where(valid, wave_buf[v, l].astype(jnp.float32), 0.0)
            masked[l, v * pad : (v + 1) * pad] = value.astype(jnp.bfloat16)

    def first_stage(l, t, u):
        product = lax.dot_general(masked[l], right_buf[l, t], NT, preferred_element_type=jnp.float32)
        half[u] = product.astype(jnp.bfloat16)

    def second_stage(l, t, u):
        place = pair_ref[l, t] - first
        flip = ((place < 0) & (z == 0)) | ((place >= sectors) & (z == Z_RUN - 1))
        near = x_lo ^ flip.astype(jnp.int32)
        blocks = [2 * near + core, 2 * (1 - near) + core, 2 * near + 1 - core, 2 * (1 - near) + 1 - core]
        lhs = jnp.concatenate(
            [left_buf[l, t, pl.ds(pl.multiple_of(b * run, run), run), :] for b in blocks], axis=0
        )
        for v, (keep, send) in enumerate(((keep0, send0), (keep1, send1))):
            term = lax.dot_general(lhs, half[u, v * pad : (v + 1) * pad], NN, preferred_element_type=jnp.float32)
            for q in range(2):
                keep[place + sectors, q] += term[q * run : (q + 1) * run]
                send[place + sectors, q] += term[(2 + q) * run : (3 + q) * run]

    dims_copy.wait()
    own_rows = lax.broadcasted_iota(jnp.int32, (run, pad), 0) + ops * run
    own_cols = lax.broadcasted_iota(jnp.int32, (run, pad), 1)
    for l in range(sectors):
        valid = (own_rows < dims_ref[0, first + l]) & (own_cols < dims_ref[1, first + l])
        inside[l] = jnp.where(valid, 1.0, 0.0)
    pair_copy.wait()
    for i, (l, t, number) in enumerate(parts):
        if t == 0:
            wave_copy(l).wait()
        right_copy(i).wait()
        left_copy(i).wait()
        if t == 0:
            mask(l)
        first_stage(l, t, 0)
        for u in range(number):
            if u + 1 < number:
                first_stage(l, t + u + 1, u + 1)
            second_stage(l, t + u, u)


def terms_call(me, dims, pairing, wave, left, right):
    terms, sectors, pad, _ = left.shape
    pairs = terms * sectors
    shape = jax.ShapeDtypeStruct((3 * sectors, 2, pad // 4, pad), jnp.float32)
    in_hbm = pl.BlockSpec(memory_space=pltpu.HBM)
    vmem = pl.BlockSpec(memory_space=pltpu.VMEM)
    operands = (dims, pairing.T, wave, left, right)
    return pl.pallas_call(
        terms_kernel,
        out_shape=(shape,) * 4 + (jax.ShapeDtypeStruct((sectors, pad // 4, pad), jnp.float32),),
        in_specs=[pl.BlockSpec(memory_space=pltpu.SMEM)] + [in_hbm] * 5,
        out_specs=(vmem,) * 5,
        scratch_shapes=[
            pltpu.VMEM(wave.shape, jnp.bfloat16),
            pltpu.VMEM((sectors, 2 * pad, pad), jnp.bfloat16),
            pltpu.VMEM((sectors, terms, pad, pad), jnp.bfloat16),
            pltpu.VMEM((sectors, terms, pad, pad), jnp.bfloat16),
            pltpu.VMEM((terms, 2 * pad, pad), jnp.bfloat16),
            pltpu.SMEM(dims.shape, jnp.int32),
            pltpu.SMEM((sectors, terms), jnp.int32),
            pltpu.SemaphoreType.DMA((sectors,)),
            pltpu.SemaphoreType.DMA((sectors + 1,)),
            pltpu.SemaphoreType.DMA((sectors + 1,)),
            pltpu.SemaphoreType.DMA,
            pltpu.SemaphoreType.DMA,
        ],
        compiler_params=pltpu.CompilerParams(vmem_limit_bytes=32 * 1024 * 1024),
        cost_estimate=pl.CostEstimate(
            flops=pairs * 8 * pad**3, bytes_accessed=pairs * pad * pad * 4, transcendentals=0
        ),
        name="terms",
    )(me.reshape(1), *(pltpu.with_memory_space_constraint(x, pltpu.HBM) for x in operands))


def small_call(kernel, name, out_shapes, *args):
    shapes = tuple(jax.ShapeDtypeStruct(s, jnp.float32) for s in out_shapes)
    size = sum(4 * x.size for x in args)
    vmem = pl.BlockSpec(memory_space=pltpu.VMEM)
    result = pl.pallas_call(
        kernel,
        out_shape=shapes,
        in_specs=[vmem] * len(args),
        out_specs=(vmem,) * len(shapes),
        compiler_params=pltpu.CompilerParams(vmem_limit_bytes=8 * 1024 * 1024),
        cost_estimate=pl.CostEstimate(flops=size // 4, bytes_accessed=size, transcendentals=0),
        name=name,
    )(*args)
    return result if len(shapes) > 1 else result[0]


def split_kernel(keep, got, down, up):
    sectors = down.shape[0]
    down[...] = keep[:sectors] + got[:sectors]
    up[...] = keep[2 * sectors :] + got[2 * sectors :]


def far_kernel(keep, got, halo, own):
    sectors = own.shape[0]
    halo[:sectors] = keep[:sectors, 1] + got[:sectors, 1]
    halo[sectors:] = keep[2 * sectors :, 1] + got[2 * sectors :, 1]
    own[...] = keep[sectors : 2 * sectors, 1] + got[sectors : 2 * sectors, 1]


def near_kernel(keep, got, far, down, up):
    sectors = down.shape[0]
    down[...] = keep[:sectors, 0] + got[:sectors, 0] + far[:sectors]
    up[...] = keep[2 * sectors :, 0] + got[2 * sectors :, 0] + far[sectors:]


def add_kernel(a, b, out):
    out[...] = a[...] + b[...]


def own_far_kernel(keep, got, both, out):
    sectors = out.shape[0]
    out[...] = keep[sectors : 2 * sectors, 1] + got[sectors : 2 * sectors, 1] + both[:, 1]


def finish_kernel(keep0, got0, both0, far0, keep1, got1, own_far1, below1, above1, inside, out):
    sectors = out.shape[1]
    for l in range(sectors):
        s = sectors + l
        valid = inside[l] > 0.0
        out[0, l] = jnp.where(valid, keep0[s, 0] + got0[s, 0] + both0[l, 0] + far0[l], 0.0)
        out[1, l] = jnp.where(valid, keep1[s, 0] + got1[s, 0] + own_far1[l] + below1[l] + above1[l], 0.0)


def body(wavefunction, left_blocks, right_blocks, pairing, sector_dims):
    sectors, pad = wavefunction.shape[1:3]
    run = pad // 4
    peers = lax.axis_size("sec")
    other_core = [(i, i ^ 1) for i in range(4)]
    other_chip = [(i, i ^ 2) for i in range(4)]
    upward = [
        (o * peers + s, (o ^ 2 if s % Z_RUN == Z_RUN - 1 else o) * peers + (s + 1) % peers)
        for o in range(4)
        for s in range(peers)
    ]
    downward = [(b, a) for a, b in upward]
    near, both = (sectors, run, pad), (sectors, 2, run, pad)

    def to_core(x):
        return lax.ppermute(x, "ops", other_core)

    def to_chip(x):
        return lax.ppermute(x, "ops", other_chip)

    def to_sector(down, up):
        return lax.ppermute(up, BOTH, upward), lax.ppermute(down, BOTH, downward)

    keep0, send0, keep1, send1, inside = terms_call(
        lax.axis_index(BOTH), sector_dims, pairing, wavefunction, left_blocks, right_blocks
    )
    got1 = to_core(send1)
    got0 = to_core(send0)
    far1, own_far1 = small_call(far_kernel, "far1", ((2 * sectors, run, pad), near), keep1, got1)
    got0, far1 = lax.optimization_barrier((got0, far1))
    far1 = to_chip(far1)
    down0, up0 = small_call(split_kernel, "split0", (both, both), keep0, got0)
    below0, above0 = to_sector(down0, up0)
    far1, own_far1 = lax.optimization_barrier((far1, own_far1))
    down1, up1 = small_call(near_kernel, "near1", (near, near), keep1, got1, far1)
    below1, above1 = to_sector(down1, up1)
    own_far1 = to_chip(own_far1)
    both0 = small_call(add_kernel, "both0", (both,), below0, above0)
    far0 = to_chip(small_call(own_far_kernel, "own_far0", (near,), keep0, got0, both0))
    return small_call(
        finish_kernel, "finish", ((2, sectors, run, pad),),
        keep0, got0, both0, far0, keep1, got1, own_far1, below1, above1, inside,
    )


def solution(mesh):
    placed = (
        P(None, "sec", None, None),
        P("ops", "sec", None, None),
        P("ops", "sec", None, None),
        P("ops", "sec"),
        P(),
    )
    return jax.shard_map(
        body, mesh=mesh, in_specs=placed, out_specs=P(None, "sec", "ops", None), check_vma=False
    )
```

```python
import functools

import jax
import jax.numpy as jnp
from jax import lax
from jax.experimental import pallas as pl
from jax.experimental.pallas import tpu as pltpu
from jax.sharding import PartitionSpec as P

Z_RUN = 8
BOTH = ("ops", "sec")
WEIGHTY = ("base0", "base1", "sum1", "up1")
EARLY = 2
NT = (((1,), (1,)), ((), ()))
NN = (((1,), (0,)), ((), ()))


def terms_kernel(
    me_ref, dims_hbm, pair_hbm, wave_ref, left_ref, right_ref,
    keep0, keep1, send0, send1, send_own, inside,
    wave_buf, masked, left_buf, right_buf, half, sums, dims_ref, pair_ref,
    wave_sem, left_sem, right_sem, dims_sem, pair_sem,
):
    terms, sectors, pad, _ = left_ref.shape
    run = pad // 4
    peers = dims_ref.shape[1] // sectors
    me = me_ref[0]
    sec, ops = me % peers, me // peers
    core, x_lo = ops % 2, ops // 2
    first = sec * sectors
    z = sec % Z_RUN

    pair_copy = pltpu.make_async_copy(pair_hbm, pair_ref, pair_sem)
    dims_copy = pltpu.make_async_copy(dims_hbm, dims_ref, dims_sem)
    parts = [(0, 0, EARLY), (0, EARLY, terms - EARLY)] + [(l, 0, terms) for l in range(1, sectors)]

    def wave_copy(l):
        return pltpu.make_async_copy(wave_ref.at[:, l], wave_buf.at[:, l], wave_sem.at[l])

    def right_copy(i):
        l, t, number = parts[i]
        at = pl.ds(t, number)
        return pltpu.make_async_copy(right_ref.at[at, l], right_buf.at[l, at], right_sem.at[i])

    def left_copy(i):
        l, t, number = parts[i]
        at = pl.ds(t, number)
        return pltpu.make_async_copy(left_ref.at[at, l], left_buf.at[l, at], left_sem.at[i])

    dims_copy.start()
    pair_copy.start()
    wave_copy(0).start()
    right_copy(0).start()
    left_copy(0).start()
    for i in range(1, len(parts)):
        if i < sectors:
            wave_copy(i).start(priority=1)
        right_copy(i).start(priority=1)
        left_copy(i).start(priority=1)

    for ref in (keep0, keep1, sums):
        ref[...] = jnp.zeros_like(ref)
    rows = lax.broadcasted_iota(jnp.int32, (pad, pad), 0)
    cols = lax.broadcasted_iota(jnp.int32, (pad, pad), 1)

    def mask(l):
        valid = (rows < dims_ref[0, first + l]) & (cols < dims_ref[1, first + l])
        for v in range(2):
            value = jnp.where(valid, wave_buf[v, l].astype(jnp.float32), 0.0)
            masked[l, v * pad : (v + 1) * pad] = value.astype(jnp.bfloat16)

    def first_stage(l, t, u):
        product = lax.dot_general(masked[l], right_buf[l, t], NT, preferred_element_type=jnp.float32)
        half[u] = product.astype(jnp.bfloat16)

    def second_stage(l, t, u):
        place = pair_ref[l, t] - first
        flip = ((place < 0) & (z == 0)) | ((place >= sectors) & (z == Z_RUN - 1))
        near = x_lo ^ flip.astype(jnp.int32)
        blocks = [2 * near + core, 2 * (1 - near) + core, 2 * near + 1 - core, 2 * (1 - near) + 1 - core]
        lhs = jnp.concatenate(
            [left_buf[l, t, pl.ds(pl.multiple_of(b * run, run), run), :] for b in blocks], axis=0
        )
        for v, keep in enumerate((keep0, keep1)):
            term = lax.dot_general(lhs, half[u, v * pad : (v + 1) * pad], NN, preferred_element_type=jnp.float32)
            for q in range(2):
                keep[place + sectors, q] += term[q * run : (q + 1) * run]
                sums[v, place + sectors, q] += term[(2 + q) * run : (3 + q) * run]

    dims_copy.wait()
    own_rows = lax.broadcasted_iota(jnp.int32, (run, pad), 0) + ops * run
    own_cols = lax.broadcasted_iota(jnp.int32, (run, pad), 1)
    for l in range(sectors):
        valid = (own_rows < dims_ref[0, first + l]) & (own_cols < dims_ref[1, first + l])
        inside[l] = jnp.where(valid, 1.0, 0.0)
    pair_copy.wait()
    for i, (l, t, number) in enumerate(parts):
        if t == 0:
            wave_copy(l).wait()
        right_copy(i).wait()
        left_copy(i).wait()
        if t == 0:
            mask(l)
        first_stage(l, t, 0)
        for u in range(number):
            if u + 1 < number:
                first_stage(l, t + u + 1, u + 1)
            second_stage(l, t + u, u)
    for v, send in enumerate((send0, send1)):
        send[:sectors] = sums[v, :sectors]
        send[sectors:] = sums[v, 2 * sectors :]
    send_own[...] = sums[:, sectors : 2 * sectors]


def terms_call(me, dims, pairing, wave, left, right):
    terms, sectors, pad, _ = left.shape
    pairs = terms * sectors
    def shape(*leading):
        return jax.ShapeDtypeStruct((*leading, pad // 4, pad), jnp.float32)

    in_hbm = pl.BlockSpec(memory_space=pltpu.HBM)
    vmem = pl.BlockSpec(memory_space=pltpu.VMEM)
    operands = (dims, pairing.T, wave, left, right)
    return pl.pallas_call(
        terms_kernel,
        out_shape=(
            shape(3 * sectors, 2), shape(3 * sectors, 2), shape(2 * sectors, 2), shape(2 * sectors, 2),
            shape(2, sectors, 2), shape(sectors),
        ),
        in_specs=[pl.BlockSpec(memory_space=pltpu.SMEM)] + [in_hbm] * 5,
        out_specs=(vmem,) * 6,
        scratch_shapes=[
            pltpu.VMEM(wave.shape, jnp.bfloat16),
            pltpu.VMEM((sectors, 2 * pad, pad), jnp.bfloat16),
            pltpu.VMEM((sectors, terms, pad, pad), jnp.bfloat16),
            pltpu.VMEM((sectors, terms, pad, pad), jnp.bfloat16),
            pltpu.VMEM((terms, 2 * pad, pad), jnp.bfloat16),
            pltpu.VMEM((2, 3 * sectors, 2, pad // 4, pad), jnp.float32),
            pltpu.SMEM(dims.shape, jnp.int32),
            pltpu.SMEM((sectors, terms), jnp.int32),
            pltpu.SemaphoreType.DMA((sectors,)),
            pltpu.SemaphoreType.DMA((sectors + 1,)),
            pltpu.SemaphoreType.DMA((sectors + 1,)),
            pltpu.SemaphoreType.DMA,
            pltpu.SemaphoreType.DMA,
        ],
        compiler_params=pltpu.CompilerParams(vmem_limit_bytes=32 * 1024 * 1024),
        cost_estimate=pl.CostEstimate(
            flops=pairs * 8 * pad**3, bytes_accessed=pairs * pad * pad * 4, transcendentals=0
        ),
        name="terms",
    )(me.reshape(1), *(pltpu.with_memory_space_constraint(x, pltpu.HBM) for x in operands))


def small_call(kernel, name, out_shapes, *args):
    shapes = tuple(jax.ShapeDtypeStruct(s, jnp.float32) for s in out_shapes)
    size = (40 if name in WEIGHTY else 1) * sum(4 * x.size for x in args)
    vmem = pl.BlockSpec(memory_space=pltpu.VMEM)
    result = pl.pallas_call(
        kernel,
        out_shape=shapes,
        in_specs=[vmem] * len(args),
        out_specs=(vmem,) * len(shapes),
        compiler_params=pltpu.CompilerParams(vmem_limit_bytes=8 * 1024 * 1024),
        cost_estimate=pl.CostEstimate(flops=size // 4, bytes_accessed=size, transcendentals=0),
        name=name,
    )(*args)
    return result if len(shapes) > 1 else result[0]


def up_kernel(keep, got, out):
    sectors = out.shape[0]
    out[...] = keep[2 * sectors :] + got[sectors:]


def down_kernel(keep, got, out):
    sectors = out.shape[0]
    out[...] = keep[:sectors] + got[:sectors]


def far_kernel(keep, got, out):
    sectors = out.shape[0] // 2
    out[:sectors] = keep[:sectors, 1] + got[:sectors, 1]
    out[sectors:] = keep[2 * sectors :, 1] + got[sectors:, 1]


def near_up_kernel(keep, got, far, out):
    sectors = out.shape[0]
    out[...] = keep[2 * sectors :, 0] + got[sectors:, 0] + far[sectors:]


def near_down_kernel(keep, got, far, out):
    sectors = out.shape[0]
    out[...] = keep[:sectors, 0] + got[:sectors, 0] + far[:sectors]


def own_far1_kernel(keep, got, out):
    sectors = out.shape[0]
    out[...] = keep[sectors : 2 * sectors, 1] + got[1, :, 1]


def base0_kernel(keep, got, below, out):
    sectors = out.shape[0]
    out[...] = keep[sectors : 2 * sectors] + got[0] + below[...]


def own_far0_kernel(base, above, out):
    out[...] = base[:, 1] + above[:, 1]


def base1_kernel(keep, got, far, below, out):
    sectors = out.shape[0]
    out[...] = keep[sectors : 2 * sectors, 0] + got[1, :, 0] + far[...] + below[...]


def sum1_kernel(base, above, out):
    out[...] = base[...] + above[...]


def finish_kernel(base0, above0, far0, base1, inside, out):
    for l in range(out.shape[1]):
        valid = inside[l] > 0.0
        out[0, l] = jnp.where(valid, base0[l, 0] + above0[l, 0] + far0[l], 0.0)
        out[1, l] = jnp.where(valid, base1[l], 0.0)


def body(wavefunction, left_blocks, right_blocks, pairing, sector_dims):
    sectors, pad = wavefunction.shape[1:3]
    run = pad // 4
    peers = lax.axis_size("sec")
    other_core = [(i, i ^ 1) for i in range(4)]
    other_chip = [(i, i ^ 2) for i in range(4)]
    upward = [
        (o * peers + s, (o ^ 2 if s % Z_RUN == Z_RUN - 1 else o) * peers + (s + 1) % peers)
        for o in range(4)
        for s in range(peers)
    ]
    downward = [(b, a) for a, b in upward]
    near, both = (sectors, run, pad), (sectors, 2, run, pad)

    def to_core(x):
        return lax.ppermute(x, "ops", other_core)

    def to_chip(x):
        return lax.ppermute(x, "ops", other_chip)

    def to_above(x):
        return lax.ppermute(x, BOTH, upward)

    def to_below(x):
        return lax.ppermute(x, BOTH, downward)

    def after(first, second):
        return lax.optimization_barrier((first, second))

    keep0, keep1, send0, send1, send_own, inside = terms_call(
        lax.axis_index(BOTH), sector_dims, pairing, wavefunction, left_blocks, right_blocks
    )
    got1 = to_core(send1)
    got = to_core(send_own)

    far1 = small_call(far_kernel, "far1", ((2 * sectors, run, pad),), keep1, got1)
    far1, send0 = after(far1, send0)
    got0 = to_core(send0)
    far1 = to_chip(far1)
    below0 = to_above(small_call(up_kernel, "up0", (both,), keep0, got0))
    above0 = to_below(small_call(down_kernel, "down0", (both,), keep0, got0))

    below1 = to_above(small_call(near_up_kernel, "up1", (near,), keep1, got1, far1))
    far1_later, got_later = after(far1, got)
    own_far1 = small_call(own_far1_kernel, "own_far1", (near,), keep1, got_later)
    base0 = small_call(base0_kernel, "base0", (both,), keep0, got, below0)
    far0 = small_call(own_far0_kernel, "own_far0", (near,), base0, above0)
    own_far1, far1_later = after(own_far1, far1)
    above1 = to_below(small_call(near_down_kernel, "down1", (near,), keep1, got1, far1_later))
    own_far1 = to_chip(own_far1)
    far0 = to_chip(far0)
    base1 = small_call(base1_kernel, "base1", (near,), keep1, got, own_far1, below1)
    sum1 = small_call(sum1_kernel, "sum1", (near,), base1, above1)
    return small_call(finish_kernel, "finish", ((2, sectors, run, pad),), base0, above0, far0, sum1, inside)


def solution(mesh):
    placed = (
        P(None, "sec", None, None),
        P("ops", "sec", None, None),
        P("ops", "sec", None, None),
        P("ops", "sec"),
        P(),
    )
    return jax.shard_map(
        body, mesh=mesh, in_specs=placed, out_specs=P(None, "sec", "ops", None), check_vma=False
    )
```

```python
import functools

import jax
import jax.numpy as jnp
from jax import lax
from jax.experimental import pallas as pl
from jax.experimental.pallas import tpu as pltpu
from jax.sharding import PartitionSpec as P

Z_RUN = 8
BOTH = ("ops", "sec")
WEIGHTY = ("base0", "base1", "sum1", "up1")
EARLY = 2
NT = (((1,), (1,)), ((), ()))
NN = (((1,), (0,)), ((), ()))


def own_place(me_ref, peers, sectors):
    sec, ops = me_ref[0] % peers, me_ref[0] // peers
    return ops % 2, ops // 2, sec * sectors, sec % Z_RUN


def add_terms(parts, wait, place_of, keep, sums, masked, left_buf, right_buf, half, core, x_lo, z):
    sectors, terms, pad, _ = left_buf.shape
    run = pad // 4

    def first_stage(l, t, u):
        product = lax.dot_general(masked[l], right_buf[l, t], NT, preferred_element_type=jnp.float32)
        half[u] = product.astype(jnp.bfloat16)

    def second_stage(l, t, u):
        place = place_of(l, t)
        flip = ((place < 0) & (z == 0)) | ((place >= sectors) & (z == Z_RUN - 1))
        near = x_lo ^ flip.astype(jnp.int32)
        blocks = [2 * near + core, 2 * (1 - near) + core, 2 * near + 1 - core, 2 * (1 - near) + 1 - core]
        lhs = jnp.concatenate(
            [left_buf[l, t, pl.ds(pl.multiple_of(b * run, run), run), :] for b in blocks], axis=0
        )
        term = lax.dot_general(lhs, half[u], NN, preferred_element_type=jnp.float32)
        for q in range(2):
            keep[place + sectors, q] += term[q * run : (q + 1) * run]
            sums[place + sectors, q] += term[(2 + q) * run : (3 + q) * run]

    for i, (l, t, number) in enumerate(parts):
        wait(i, l, t)
        first_stage(l, t, 0)
        for u in range(number):
            if u + 1 < number:
                first_stage(l, t + u + 1, u + 1)
            second_stage(l, t + u, u)


def give_sums(sums, send, send_own):
    sectors = send_own.shape[0]
    send[:sectors] = sums[:sectors]
    send[sectors:] = sums[2 * sectors :]
    send_own[...] = sums[sectors : 2 * sectors]


def terms1_kernel(
    me_ref, dims_hbm, pair_hbm, wave_ref, left_ref, right_ref,
    keep, send, send_own, inside, left_buf, right_buf, masked0,
    wave_buf, masked1, half, sums, dims_ref, pair_ref,
    wave_sem, left_sem, right_sem, dims_sem, pair_sem,
):
    terms, sectors, pad, _ = left_ref.shape
    run = pad // 4
    peers = dims_ref.shape[1] // sectors
    core, x_lo, first, z = own_place(me_ref, peers, sectors)
    ops = me_ref[0] // peers

    pair_copy = pltpu.make_async_copy(pair_hbm, pair_ref, pair_sem)
    dims_copy = pltpu.make_async_copy(dims_hbm, dims_ref, dims_sem)
    parts = [(0, 0, EARLY), (0, EARLY, terms - EARLY)] + [(l, 0, terms) for l in range(1, sectors)]

    def wave_copy(l):
        return pltpu.make_async_copy(wave_ref.at[:, l], wave_buf.at[:, l], wave_sem.at[l])

    def right_copy(i):
        l, t, number = parts[i]
        at = pl.ds(t, number)
        return pltpu.make_async_copy(right_ref.at[at, l], right_buf.at[l, at], right_sem.at[i])

    def left_copy(i):
        l, t, number = parts[i]
        at = pl.ds(t, number)
        return pltpu.make_async_copy(left_ref.at[at, l], left_buf.at[l, at], left_sem.at[i])

    dims_copy.start()
    pair_copy.start()
    wave_copy(0).start()
    right_copy(0).start()
    left_copy(0).start()
    for i in range(1, len(parts)):
        if i < sectors:
            wave_copy(i).start(priority=1)
        right_copy(i).start(priority=1)
        left_copy(i).start(priority=1)

    for ref in (keep, sums):
        ref[...] = jnp.zeros_like(ref)
    rows = lax.broadcasted_iota(jnp.int32, (pad, pad), 0)
    cols = lax.broadcasted_iota(jnp.int32, (pad, pad), 1)

    def mask(l):
        valid = (rows < dims_ref[0, first + l]) & (cols < dims_ref[1, first + l])
        for v, masked in enumerate((masked0, masked1)):
            masked[l] = jnp.where(valid, wave_buf[v, l].astype(jnp.float32), 0.0).astype(jnp.bfloat16)

    dims_copy.wait()
    own_rows = lax.broadcasted_iota(jnp.int32, (run, pad), 0) + ops * run
    own_cols = lax.broadcasted_iota(jnp.int32, (run, pad), 1)
    for l in range(sectors):
        valid = (own_rows < dims_ref[0, first + l]) & (own_cols < dims_ref[1, first + l])
        inside[l] = jnp.where(valid, 1.0, 0.0)
    pair_copy.wait()

    def wait(i, l, t):
        if t == 0:
            wave_copy(l).wait()
        right_copy(i).wait()
        left_copy(i).wait()
        if t == 0:
            mask(l)

    add_terms(
        parts, wait, lambda l, t: pair_ref[l, t] - first, keep, sums, masked1, left_buf, right_buf, half, core, x_lo, z
    )
    give_sums(sums, send, send_own)


def terms0_kernel(peers, me_ref, pair_hbm, left_buf, right_buf, masked0, keep, send, send_own, half, sums, pair_ref, pair_sem):
    sectors, terms, pad, _ = left_buf.shape
    core, x_lo, first, z = own_place(me_ref, peers, sectors)
    pair_copy = pltpu.make_async_copy(pair_hbm, pair_ref, pair_sem)
    pair_copy.start()
    for ref in (keep, sums):
        ref[...] = jnp.zeros_like(ref)
    pair_copy.wait()
    add_terms(
        [(l, 0, terms) for l in range(sectors)], lambda i, l, t: None, lambda l, t: pair_ref[l, t] - first,
        keep, sums, masked0, left_buf, right_buf, half, core, x_lo, z,
    )
    give_sums(sums, send, send_own)


def terms_calls(me, dims, pairing, wave, left, right):
    terms, sectors, pad, _ = left.shape
    pairs = terms * sectors
    peers = dims.shape[1] // sectors

    def shape(*leading):
        return jax.ShapeDtypeStruct((*leading, pad // 4, pad), jnp.float32)

    def half_shape(*leading):
        return jax.ShapeDtypeStruct((*leading, pad, pad), jnp.bfloat16)

    sums = (shape(3 * sectors, 2), shape(2 * sectors, 2), shape(sectors, 2))
    in_hbm = pl.BlockSpec(memory_space=pltpu.HBM)
    in_smem = pl.BlockSpec(memory_space=pltpu.SMEM)
    vmem = pl.BlockSpec(memory_space=pltpu.VMEM)
    me = me.reshape(1)
    operands = [pltpu.with_memory_space_constraint(x, pltpu.HBM) for x in (dims, pairing.T, wave, left, right)]
    sums_buf = pltpu.VMEM((3 * sectors, 2, pad // 4, pad), jnp.float32)
    half_buf = pltpu.VMEM((terms, pad, pad), jnp.bfloat16)
    cost = pl.CostEstimate(flops=pairs * 4 * pad**3, bytes_accessed=pairs * pad * pad * 4, transcendentals=0)
    keep1, send1, own1, inside, left, right, masked0 = pl.pallas_call(
        terms1_kernel,
        out_shape=(
            *sums, shape(sectors), half_shape(sectors, terms), half_shape(sectors, terms), half_shape(sectors)
        ),
        in_specs=[in_smem] + [in_hbm] * 5,
        out_specs=(vmem,) * 7,
        scratch_shapes=[
            pltpu.VMEM(wave.shape, jnp.bfloat16),
            pltpu.VMEM((sectors, pad, pad), jnp.bfloat16),
            half_buf,
            sums_buf,
            pltpu.SMEM(dims.shape, jnp.int32),
            pltpu.SMEM((sectors, terms), jnp.int32),
            pltpu.SemaphoreType.DMA((sectors,)),
            pltpu.SemaphoreType.DMA((sectors + 1,)),
            pltpu.SemaphoreType.DMA((sectors + 1,)),
            pltpu.SemaphoreType.DMA,
            pltpu.SemaphoreType.DMA,
        ],
        compiler_params=pltpu.CompilerParams(vmem_limit_bytes=24 * 1024 * 1024),
        cost_estimate=cost,
        name="terms1",
    )(me, *operands)
    keep0, send0, own0 = pl.pallas_call(
        functools.partial(terms0_kernel, peers),
        out_shape=sums,
        in_specs=[in_smem, in_hbm, vmem, vmem, vmem],
        out_specs=(vmem,) * 3,
        scratch_shapes=[half_buf, sums_buf, pltpu.SMEM((sectors, terms), jnp.int32), pltpu.SemaphoreType.DMA],
        compiler_params=pltpu.CompilerParams(vmem_limit_bytes=24 * 1024 * 1024),
        cost_estimate=cost,
        name="terms0",
    )(me, operands[1], left, right, masked0)
    return (keep0, send0, own0), (keep1, send1, own1), inside


def small_call(kernel, name, out_shapes, *args):
    shapes = tuple(jax.ShapeDtypeStruct(s, jnp.float32) for s in out_shapes)
    size = (40 if name in WEIGHTY else 1) * sum(4 * x.size for x in args)
    vmem = pl.BlockSpec(memory_space=pltpu.VMEM)
    result = pl.pallas_call(
        kernel,
        out_shape=shapes,
        in_specs=[vmem] * len(args),
        out_specs=(vmem,) * len(shapes),
        compiler_params=pltpu.CompilerParams(vmem_limit_bytes=8 * 1024 * 1024),
        cost_estimate=pl.CostEstimate(flops=size // 4, bytes_accessed=size, transcendentals=0),
        name=name,
    )(*args)
    return result if len(shapes) > 1 else result[0]


def up_kernel(keep, got, out):
    sectors = out.shape[0]
    out[...] = keep[2 * sectors :] + got[sectors:]


def down_kernel(keep, got, out):
    sectors = out.shape[0]
    out[...] = keep[:sectors] + got[:sectors]


def far_kernel(keep, got, out):
    sectors = out.shape[0] // 2
    out[:sectors] = keep[:sectors, 1] + got[:sectors, 1]
    out[sectors:] = keep[2 * sectors :, 1] + got[sectors:, 1]


def near_up_kernel(keep, got, far, out):
    sectors = out.shape[0]
    out[...] = keep[2 * sectors :, 0] + got[sectors:, 0] + far[sectors:]


def near_down_kernel(keep, got, far, out):
    sectors = out.shape[0]
    out[...] = keep[:sectors, 0] + got[:sectors, 0] + far[:sectors]


def own_far1_kernel(keep, got, out):
    sectors = out.shape[0]
    out[...] = keep[sectors : 2 * sectors, 1] + got[:, 1]


def base0_kernel(keep, got, below, out):
    sectors = out.shape[0]
    out[...] = keep[sectors : 2 * sectors] + got[...] + below[...]


def own_far0_kernel(base, above, out):
    out[...] = base[:, 1] + above[:, 1]


def base1_kernel(keep, got, far, below, out):
    sectors = out.shape[0]
    out[...] = keep[sectors : 2 * sectors, 0] + got[:, 0] + far[...] + below[...]


def sum1_kernel(base, above, out):
    out[...] = base[...] + above[...]


def finish_kernel(base0, above0, far0, base1, inside, out):
    for l in range(out.shape[1]):
        valid = inside[l] > 0.0
        out[0, l] = jnp.where(valid, base0[l, 0] + above0[l, 0] + far0[l], 0.0)
        out[1, l] = jnp.where(valid, base1[l], 0.0)


def body(wavefunction, left_blocks, right_blocks, pairing, sector_dims):
    sectors, pad = wavefunction.shape[1:3]
    run = pad // 4
    peers = lax.axis_size("sec")
    other_core = [(i, i ^ 1) for i in range(4)]
    other_chip = [(i, i ^ 2) for i in range(4)]
    upward = [
        (o * peers + s, (o ^ 2 if s % Z_RUN == Z_RUN - 1 else o) * peers + (s + 1) % peers)
        for o in range(4)
        for s in range(peers)
    ]
    downward = [(b, a) for a, b in upward]
    near, both = (sectors, run, pad), (sectors, 2, run, pad)

    def to_core(x):
        return lax.ppermute(x, "ops", other_core)

    def to_chip(x):
        return lax.ppermute(x, "ops", other_chip)

    def to_above(x):
        return lax.ppermute(x, BOTH, upward)

    def to_below(x):
        return lax.ppermute(x, BOTH, downward)

    def after(first, second):
        return lax.optimization_barrier((first, second))

    (keep0, send0, send_own0), (keep1, send1, send_own1), inside = terms_calls(
        lax.axis_index(BOTH), sector_dims, pairing, wavefunction, left_blocks, right_blocks
    )
    got1 = to_core(send1)

    far1 = small_call(far_kernel, "far1", ((2 * sectors, run, pad),), keep1, got1)
    far1, send0 = after(far1, send0)
    got0 = to_core(send0)
    far1 = to_chip(far1)
    below0 = to_above(small_call(up_kernel, "up0", (both,), keep0, got0))
    down0 = small_call(down_kernel, "down0", (both,), keep0, got0)
    down0, (send_own1, send_own0) = after(down0, (send_own1, send_own0))
    above0 = to_below(down0)
    own_got1 = to_core(send_own1)
    own_got0 = to_core(send_own0)

    below1 = to_above(small_call(near_up_kernel, "up1", (near,), keep1, got1, far1))
    far1_later, got_later = after(far1, own_got1)
    own_far1 = small_call(own_far1_kernel, "own_far1", (near,), keep1, got_later)
    base0 = small_call(base0_kernel, "base0", (both,), keep0, own_got0, below0)
    far0 = small_call(own_far0_kernel, "own_far0", (near,), base0, above0)
    own_far1, far1_later = after(own_far1, far1)
    above1 = to_below(small_call(near_down_kernel, "down1", (near,), keep1, got1, far1_later))
    own_far1 = to_chip(own_far1)
    far0 = to_chip(far0)
    base1 = small_call(base1_kernel, "base1", (near,), keep1, own_got1, own_far1, below1)
    sum1 = small_call(sum1_kernel, "sum1", (near,), base1, above1)
    return small_call(finish_kernel, "finish", ((2, sectors, run, pad),), base0, above0, far0, sum1, inside)


def solution(mesh):
    placed = (
        P(None, "sec", None, None),
        P("ops", "sec", None, None),
        P("ops", "sec", None, None),
        P("ops", "sec"),
        P(),
    )
    return jax.shard_map(
        body, mesh=mesh, in_specs=placed, out_specs=P(None, "sec", "ops", None), check_vma=False
    )
```

```python
import functools

import jax
import jax.numpy as jnp
from jax import lax
from jax.experimental import pallas as pl
from jax.experimental.pallas import tpu as pltpu
from jax.sharding import PartitionSpec as P

Z_RUN = 8
BOTH = ("ops", "sec")
WEIGHTY = ("base0", "base1", "sum1", "up1")
EARLY = 2
NT = (((1,), (1,)), ((), ()))
NN = (((1,), (0,)), ((), ()))


def own_place(me_ref, peers, sectors):
    sec, ops = me_ref[0] % peers, me_ref[0] // peers
    return ops % 2, ops // 2, sec * sectors, sec % Z_RUN


def add_terms(parts, wait, place_of, keep, sums, masked, left_buf, right_buf, half, core, x_lo, z):
    sectors, terms, pad, _ = left_buf.shape
    run = pad // 4

    def first_stage(l, t, u):
        product = lax.dot_general(masked[l], right_buf[l, t], NT, preferred_element_type=jnp.float32)
        half[u] = product.astype(jnp.bfloat16)

    def second_stage(l, t, u):
        place = place_of(l, t)
        flip = ((place < 0) & (z == 0)) | ((place >= sectors) & (z == Z_RUN - 1))
        near = x_lo ^ flip.astype(jnp.int32)
        blocks = [2 * near + core, 2 * (1 - near) + core, 2 * near + 1 - core, 2 * (1 - near) + 1 - core]
        lhs = jnp.concatenate(
            [left_buf[l, t, pl.ds(pl.multiple_of(b * run, run), run), :] for b in blocks], axis=0
        )
        term = lax.dot_general(lhs, half[u], NN, preferred_element_type=jnp.float32)
        for q in range(2):
            keep[place + sectors, q] += term[q * run : (q + 1) * run]
            sums[place + sectors, q] += term[(2 + q) * run : (3 + q) * run]

    for i, (l, t, number) in enumerate(parts):
        wait(i, l, t)
        first_stage(l, t, 0)
        for u in range(number):
            if u + 1 < number:
                first_stage(l, t + u + 1, u + 1)
            second_stage(l, t + u, u)


def give_sums(sums, send, send_own):
    sectors = send_own.shape[0]
    send[:sectors] = sums[:sectors]
    send[sectors:] = sums[2 * sectors :]
    send_own[...] = sums[sectors : 2 * sectors]


def terms1_kernel(
    me_ref, dims_hbm, pair_hbm, wave_ref, left_ref, right_ref,
    keep, send, send_own, inside, left_buf, right_buf, masked0,
    wave_buf, masked1, half, sums, dims_ref, pair_ref,
    wave_sem, left_sem, right_sem, dims_sem, pair_sem,
):
    terms, sectors, pad, _ = left_ref.shape
    run = pad // 4
    peers = dims_ref.shape[1] // sectors
    core, x_lo, first, z = own_place(me_ref, peers, sectors)
    ops = me_ref[0] // peers

    pair_copy = pltpu.make_async_copy(pair_hbm, pair_ref, pair_sem)
    dims_copy = pltpu.make_async_copy(dims_hbm, dims_ref, dims_sem)
    parts = [(0, 0, EARLY), (0, EARLY, terms - EARLY)] + [(l, 0, terms) for l in range(1, sectors)]

    def wave_copy(l):
        return pltpu.make_async_copy(wave_ref.at[:, l], wave_buf.at[:, l], wave_sem.at[l])

    def right_copy(i):
        l, t, number = parts[i]
        at = pl.ds(t, number)
        return pltpu.make_async_copy(right_ref.at[at, l], right_buf.at[l, at], right_sem.at[i])

    def left_copy(i):
        l, t, number = parts[i]
        at = pl.ds(t, number)
        return pltpu.make_async_copy(left_ref.at[at, l], left_buf.at[l, at], left_sem.at[i])

    dims_copy.start()
    pair_copy.start()
    wave_copy(0).start()
    right_copy(0).start()
    left_copy(0).start()
    for i in range(1, len(parts)):
        if i < sectors:
            wave_copy(i).start(priority=1)
        right_copy(i).start(priority=1)
        left_copy(i).start(priority=1)

    for ref in (keep, sums):
        ref[...] = jnp.zeros_like(ref)
    rows = lax.broadcasted_iota(jnp.int32, (pad, pad), 0)
    cols = lax.broadcasted_iota(jnp.int32, (pad, pad), 1)

    def mask(l):
        valid = (rows < dims_ref[0, first + l]) & (cols < dims_ref[1, first + l])
        for v, masked in enumerate((masked0, masked1)):
            masked[l] = jnp.where(valid, wave_buf[v, l].astype(jnp.float32), 0.0).astype(jnp.bfloat16)

    dims_copy.wait()
    own_rows = lax.broadcasted_iota(jnp.int32, (run, pad), 0) + ops * run
    own_cols = lax.broadcasted_iota(jnp.int32, (run, pad), 1)
    for l in range(sectors):
        valid = (own_rows < dims_ref[0, first + l]) & (own_cols < dims_ref[1, first + l])
        inside[l] = jnp.where(valid, 1.0, 0.0)
    pair_copy.wait()

    def wait(i, l, t):
        if t == 0:
            wave_copy(l).wait()
        right_copy(i).wait()
        left_copy(i).wait()
        if t == 0:
            mask(l)

    add_terms(
        parts, wait, lambda l, t: pair_ref[l, t] - first, keep, sums, masked1, left_buf, right_buf, half, core, x_lo, z
    )
    give_sums(sums, send, send_own)


def terms0_kernel(peers, me_ref, pair_hbm, left_buf, right_buf, masked0, keep, send, send_own, half, sums, pair_ref, pair_sem):
    sectors, terms, pad, _ = left_buf.shape
    core, x_lo, first, z = own_place(me_ref, peers, sectors)
    pair_copy = pltpu.make_async_copy(pair_hbm, pair_ref, pair_sem)
    pair_copy.start()
    for ref in (keep, sums):
        ref[...] = jnp.zeros_like(ref)
    pair_copy.wait()
    add_terms(
        [(l, 0, terms) for l in range(sectors)], lambda i, l, t: None, lambda l, t: pair_ref[l, t] - first,
        keep, sums, masked0, left_buf, right_buf, half, core, x_lo, z,
    )
    give_sums(sums, send, send_own)


def terms_calls(me, dims, pairing, wave, left, right):
    terms, sectors, pad, _ = left.shape
    pairs = terms * sectors
    peers = dims.shape[1] // sectors

    def shape(*leading):
        return jax.ShapeDtypeStruct((*leading, pad // 4, pad), jnp.float32)

    def half_shape(*leading):
        return jax.ShapeDtypeStruct((*leading, pad, pad), jnp.bfloat16)

    sums = (shape(3 * sectors, 2), shape(2 * sectors, 2), shape(sectors, 2))
    in_hbm = pl.BlockSpec(memory_space=pltpu.HBM)
    in_smem = pl.BlockSpec(memory_space=pltpu.SMEM)
    vmem = pl.BlockSpec(memory_space=pltpu.VMEM)
    me = me.reshape(1)
    operands = [pltpu.with_memory_space_constraint(x, pltpu.HBM) for x in (dims, pairing.T, wave, left, right)]
    sums_buf = pltpu.VMEM((3 * sectors, 2, pad // 4, pad), jnp.float32)
    half_buf = pltpu.VMEM((terms, pad, pad), jnp.bfloat16)
    cost = pl.CostEstimate(flops=pairs * 4 * pad**3, bytes_accessed=pairs * pad * pad * 4, transcendentals=0)
    keep1, send1, own1, inside, left, right, masked0 = pl.pallas_call(
        terms1_kernel,
        out_shape=(
            *sums, shape(sectors), half_shape(sectors, terms), half_shape(sectors, terms), half_shape(sectors)
        ),
        in_specs=[in_smem] + [in_hbm] * 5,
        out_specs=(vmem,) * 7,
        scratch_shapes=[
            pltpu.VMEM(wave.shape, jnp.bfloat16),
            pltpu.VMEM((sectors, pad, pad), jnp.bfloat16),
            half_buf,
            sums_buf,
            pltpu.SMEM(dims.shape, jnp.int32),
            pltpu.SMEM((sectors, terms), jnp.int32),
            pltpu.SemaphoreType.DMA((sectors,)),
            pltpu.SemaphoreType.DMA((sectors + 1,)),
            pltpu.SemaphoreType.DMA((sectors + 1,)),
            pltpu.SemaphoreType.DMA,
            pltpu.SemaphoreType.DMA,
        ],
        compiler_params=pltpu.CompilerParams(vmem_limit_bytes=24 * 1024 * 1024),
        cost_estimate=cost,
        name="terms1",
    )(me, *operands)
    keep0, send0, own0 = pl.pallas_call(
        functools.partial(terms0_kernel, peers),
        out_shape=sums,
        in_specs=[in_smem, in_hbm, vmem, vmem, vmem],
        out_specs=(vmem,) * 3,
        scratch_shapes=[half_buf, sums_buf, pltpu.SMEM((sectors, terms), jnp.int32), pltpu.SemaphoreType.DMA],
        compiler_params=pltpu.CompilerParams(vmem_limit_bytes=24 * 1024 * 1024),
        cost_estimate=cost,
        name="terms0",
    )(me, operands[1], left, right, masked0)
    return (keep0, send0, own0), (keep1, send1, own1), inside


def small_call(kernel, name, out_shapes, *args):
    shapes = tuple(jax.ShapeDtypeStruct(s, jnp.float32) for s in out_shapes)
    size = (40 if name in WEIGHTY else 1) * sum(4 * x.size for x in args)
    vmem = pl.BlockSpec(memory_space=pltpu.VMEM)
    result = pl.pallas_call(
        kernel,
        out_shape=shapes,
        in_specs=[vmem] * len(args),
        out_specs=(vmem,) * len(shapes),
        compiler_params=pltpu.CompilerParams(vmem_limit_bytes=8 * 1024 * 1024),
        cost_estimate=pl.CostEstimate(flops=size // 4, bytes_accessed=size, transcendentals=0),
        name=name,
    )(*args)
    return result if len(shapes) > 1 else result[0]


def up_kernel(keep, got, out):
    sectors = out.shape[0]
    out[...] = keep[2 * sectors :] + got[sectors:]


def down_kernel(keep, got, out):
    sectors = out.shape[0]
    out[...] = keep[:sectors] + got[:sectors]


def far_kernel(keep, got, out):
    sectors = out.shape[0] // 2
    out[:sectors] = keep[:sectors, 1] + got[:sectors, 1]
    out[sectors:] = keep[2 * sectors :, 1] + got[sectors:, 1]


def near_up_kernel(keep, got, far, out):
    sectors = out.shape[0]
    out[...] = keep[2 * sectors :, 0] + got[sectors:, 0] + far[sectors:]


def near_down_kernel(keep, got, far, out):
    sectors = out.shape[0]
    out[...] = keep[:sectors, 0] + got[:sectors, 0] + far[:sectors]


def own_far1_kernel(keep, got, out):
    sectors = out.shape[0]
    out[...] = keep[sectors : 2 * sectors, 1] + got[:, 1]


def base0_kernel(keep, got, below, out):
    sectors = out.shape[0]
    out[...] = keep[sectors : 2 * sectors] + got[...] + below[...]


def own_far0_kernel(base, above, out):
    out[...] = base[:, 1] + above[:, 1]


def base1_kernel(keep, got, far, below, out):
    sectors = out.shape[0]
    out[...] = keep[sectors : 2 * sectors, 0] + got[:, 0] + far[...] + below[...]


def sum1_kernel(base, above, out):
    out[...] = base[...] + above[...]


def finish_kernel(base0, above0, far0, base1, inside, out):
    for l in range(out.shape[1]):
        valid = inside[l] > 0.0
        out[0, l] = jnp.where(valid, base0[l, 0] + above0[l, 0] + far0[l], 0.0)
        out[1, l] = jnp.where(valid, base1[l], 0.0)


def body(wavefunction, left_blocks, right_blocks, pairing, sector_dims):
    sectors, pad = wavefunction.shape[1:3]
    run = pad // 4
    peers = lax.axis_size("sec")
    other_core = [(i, i ^ 1) for i in range(4)]
    other_chip = [(i, i ^ 2) for i in range(4)]
    upward = [
        (o * peers + s, (o ^ 2 if s % Z_RUN == Z_RUN - 1 else o) * peers + (s + 1) % peers)
        for o in range(4)
        for s in range(peers)
    ]
    downward = [(b, a) for a, b in upward]
    near, both = (sectors, run, pad), (sectors, 2, run, pad)

    def to_core(x):
        return lax.ppermute(x, "ops", other_core)

    def to_chip(x):
        return lax.ppermute(x, "ops", other_chip)

    def to_above(x):
        return lax.ppermute(x, BOTH, upward)

    def to_below(x):
        return lax.ppermute(x, BOTH, downward)

    def after(first, second):
        return lax.optimization_barrier((first, second))

    (keep0, send0, send_own0), (keep1, send1, send_own1), inside = terms_calls(
        lax.axis_index(BOTH), sector_dims, pairing, wavefunction, left_blocks, right_blocks
    )
    got1 = to_core(send1)
    own_got1 = to_core(send_own1)
    own_got0 = to_core(send_own0)

    got1, own_got1 = after(got1, own_got1)
    far1 = small_call(far_kernel, "far1", ((2 * sectors, run, pad),), keep1, got1)
    far1, send0 = after(far1, send0)
    got0 = to_core(send0)
    far1 = to_chip(far1)
    below0 = to_above(small_call(up_kernel, "up0", (both,), keep0, got0))
    above0 = to_below(small_call(down_kernel, "down0", (both,), keep0, got0))

    below1 = to_above(small_call(near_up_kernel, "up1", (near,), keep1, got1, far1))
    far1_later, got_later = after(far1, own_got1)
    own_far1 = small_call(own_far1_kernel, "own_far1", (near,), keep1, got_later)
    base0 = small_call(base0_kernel, "base0", (both,), keep0, own_got0, below0)
    far0 = small_call(own_far0_kernel, "own_far0", (near,), base0, above0)
    own_far1, far1_later = after(own_far1, far1)
    above1 = to_below(small_call(near_down_kernel, "down1", (near,), keep1, got1, far1_later))
    own_far1 = to_chip(own_far1)
    far0 = to_chip(far0)
    base1 = small_call(base1_kernel, "base1", (near,), keep1, own_got1, own_far1, below1)
    sum1 = small_call(sum1_kernel, "sum1", (near,), base1, above1)
    return small_call(finish_kernel, "finish", ((2, sectors, run, pad),), base0, above0, far0, sum1, inside)


def solution(mesh):
    placed = (
        P(None, "sec", None, None),
        P("ops", "sec", None, None),
        P("ops", "sec", None, None),
        P("ops", "sec"),
        P(),
    )
    return jax.shard_map(
        body, mesh=mesh, in_specs=placed, out_specs=P(None, "sec", "ops", None), check_vma=False
    )
```
